256 devices in a mesh: cd: 64 (over y, z, core), ab: 4 (over x).
Axes of the slice: x: 4, y: 4, z: 8, core: 2. Of those that a mesh axis runs over, the one named last changes fastest.
Arguments:
- amplitudes: float32 [2, 128, 458752], P(None, 'ab', 'cd'), may hold values from -16 to 16
- integrals: float32 [458752, 1536], P('cd', 'ab'), may hold values from -0.0078125 to 0.0078125
- c_index: int32 [458752], P('cd'), may hold values from 0 to 1532, as said below
- d_index: int32 [458752], P('cd'), may hold values from 0 to 1535
- a_index: int32 [1536], P('ab'), may hold values from 0 to 1532, as said below
- b_index: int32 [1536], P('ab'), may hold values from 0 to 1535
Outputs:
- ladder: float32 [128, 2, 1536], P('cd', None, 'ab')
The draws below stay inside these ranges and needn't reach their ends.
Inputs may be any that keep to these rules, and one draw needn't show every extreme that they name: c_index[p] <= d_index[p] for every pair; some pairs have c_index equal to d_index. a_index[q] <= b_index[q] for every result pair; some have a_index equal to b_index.
All inputs are finite; a program needn't handle non-finite values.
Results may differ from the reference program's by a relative error of at most 0.00007.
Values sent between devices are 32-bit elements; how exact they have to be, the bound alone decides.
No kernel may reach another device: no remote copies, remote signals or barrier semaphores. Data moves between devices by JAX's collectives and lax.ppermute only.
A program may use at most 64 MiB of HBM per device.

```python
import jax
import jax.numpy as jnp
from jax import lax

NV = 1536
IJ = 128
PAIRS = 458752
COLS = 1536


def pair_draw(key, count, salt):
    key = jax.random.fold_in(key, salt)
    first_key, off_key = jax.random.split(key)
    first = jax.random.randint(first_key, (count,), 0, NV - 3, dtype=jnp.int32)
    offset = jax.random.randint(off_key, (count,), 0, 4, dtype=jnp.int32)
    first = first.at[0].set(0).at[count - 1].set(NV - 4)
    offset = offset.at[0].set(0).at[count - 1].set(3)
    return (first, first + offset)


def draw_c_index(key, part):
    first, second = pair_draw(key, PAIRS, 11)
    return first


def draw_d_index(key, part):
    first, second = pair_draw(key, PAIRS, 11)
    return second


def draw_a_index(key, part):
    first, second = pair_draw(key, COLS, 23)
    return first


def draw_b_index(key, part):
    first, second = pair_draw(key, COLS, 23)
    return second


def with_spikes(result, rng, source, target, blocks, factor):
    owner, partner = [(jnp.arange(result.shape[position]) // (result.shape[position] // blocks)).reshape([-1 if axis == position else 1 for axis in range(result.ndim)]) for position in (source, target)]
    chosen = jax.random.permutation(rng, blocks)[partner]
    strong = (owner == chosen) | (owner == (partner + blocks // 2) % blocks)
    return jnp.where(strong, factor * result, result)


def levels(own_key, extent, cuts, smallest, top_value):
    level, own = 1.0, jax.random.fold_in(own_key, 6)
    for axis_at, blocks in cuts:
        draws = jnp.exp(jax.random.uniform(jax.random.fold_in(own, axis_at), (blocks,), jnp.float32, smallest / len(cuts), top_value / len(cuts)))
        level = level * jnp.repeat(draws, extent[axis_at] // blocks).reshape([-1 if axis == axis_at else 1 for axis in range(len(extent))])
    return level


def gaussian(stream_key, extent, scale, reach, cuts=(), held_as=jnp.bfloat16):
    drawn = jax.random.normal(stream_key, extent, jnp.float32) * scale
    if len(cuts) > 0:
        drawn = levels(stream_key, extent, cuts, -0.22, 0.18) * drawn
    return jnp.clip(drawn, min=-reach, max=reach).astype(held_as)


def heavy_noise(stream_key, shape, width, most, shards, heavy, held_as=jnp.bfloat16):
    array = width * jax.random.normal(stream_key, shape, jnp.float32)
    if shards:
        array = array * levels(stream_key, shape, shards, -0.22, 0.18)
    return jnp.clip(with_spikes(array, jax.random.fold_in(stream_key, 3), *heavy), -most, most).astype(held_as)


def setup_inputs(seed: int = 0) -> dict:
    seeds = jax.random.split(jax.random.key(seed), 7)
    amplitudes = heavy_noise(seeds[0], (2, IJ, PAIRS), 1.0, 16.0, ((1, 4), (2, 64)), (2, 1, 64, 4.0), jnp.float32)
    integrals = gaussian(seeds[1], (PAIRS, COLS), PAIRS ** -0.5, 0.0078125, ((0, 64), (1, 4)), jnp.float32)
    c_index = draw_c_index(jax.random.fold_in(seeds[6], 71), 0)
    d_index = draw_d_index(jax.random.fold_in(seeds[6], 71), 0)
    a_index = draw_a_index(jax.random.fold_in(seeds[6], 71), 0)
    b_index = draw_b_index(jax.random.fold_in(seeds[6], 71), 0)
    return dict(amplitudes=amplitudes, integrals=integrals, c_index=c_index, d_index=d_index, a_index=a_index, b_index=b_index)


def reference(amplitudes, integrals, c_index, d_index, a_index, b_index):
    same = c_index == d_index
    weight_plus = jnp.where(same, jnp.float32(0.5), jnp.float32(1.0))
    weight_minus = jnp.where(same, jnp.float32(0.0), jnp.float32(1.0))
    weights = jnp.stack([weight_plus, weight_minus])
    weighted = amplitudes * weights[:, None, :]
    summed = jnp.einsum("sip,pq->isq", weighted, integrals, precision=lax.Precision.HIGHEST)
    keep = jnp.where(a_index == b_index, jnp.float32(0.0), jnp.float32(1.0))
    factor = 0.5 * jnp.stack([jnp.ones_like(keep), keep])
    return summed * factor[None, :, :]
```

```python
import functools

import jax
import jax.numpy as jnp
from jax import lax
from jax.experimental import pallas as pl
from jax.experimental.pallas import tpu as pltpu
from jax.sharding import PartitionSpec as P

F32 = jnp.float32
BF16 = jnp.bfloat16
STEP = 1792


def halves(x):
    high = x.astype(BF16)
    return high, (x - high.astype(F32)).astype(BF16)


def products(pieces, block):
    highs, lows = zip(*[halves(piece) for piece in pieces])
    rows = sum(piece.shape[0] for piece in pieces)
    block_high, block_low = halves(block)
    high = jnp.concatenate(highs, axis=0)
    both = jnp.concatenate([high] + list(lows), axis=0)
    first = jnp.dot(both, block_high, preferred_element_type=F32)
    second = jnp.dot(high, block_low, preferred_element_type=F32)
    return first[:rows] + (first[rows:] + second)


def sum_kernel(slabs, *refs):
    piece_refs, (weight_ref, block_ref, total_ref) = refs[: len(slabs)], refs[len(slabs) :]

    @pl.when(pl.program_id(0) == 0)
    def _():
        total_ref[...] = jnp.zeros_like(total_ref)

    pieces = [ref[...] * weight_ref[slab : slab + 1, :] for ref, slab in zip(piece_refs, slabs)]
    total_ref[...] += products(pieces, block_ref[...])


def partial_sums(pieces, slabs, weights, integrals, first_step=0):
    rows = sum(piece.shape[0] for piece in pieces)
    pairs, columns = pieces[0].shape[1], integrals.shape[1]
    return pl.pallas_call(
        functools.partial(sum_kernel, slabs),
        grid=(pairs // STEP,),
        in_specs=[pl.BlockSpec((piece.shape[0], STEP), lambda k: (0, k)) for piece in pieces]
        + [
            pl.BlockSpec((2, STEP), lambda k: (0, k + first_step)),
            pl.BlockSpec((STEP, columns), lambda k: (k + first_step, 0)),
        ],
        out_specs=pl.BlockSpec((rows, columns), lambda k: (0, 0)),
        out_shape=jax.ShapeDtypeStruct((rows, columns), F32),
        compiler_params=pltpu.CompilerParams(vmem_limit_bytes=40 * 2**20),
        cost_estimate=pl.CostEstimate(
            flops=6 * rows * pairs * columns, bytes_accessed=4 * pairs * (rows + columns), transcendentals=0
        ),
    )(*pieces, weights, integrals)


def last_kernel(slabs, *refs):
    n = len(slabs)
    piece_refs, refs = refs[:n], refs[n:]
    weight_ref, block_ref, own_ref, near_ref, far_ref, opposite_ref, out_ref, total_ref = refs
    step = pl.program_id(0)

    @pl.when(step == 0)
    def _():
        total_ref[...] = opposite_ref[...]

    pieces = [ref[...] * weight_ref[slab : slab + 1, :] for ref, slab in zip(piece_refs, slabs)]
    total_ref[...] += products(pieces, block_ref[...])

    @pl.when(step == pl.num_programs(0) - 1)
    def _():
        me = lax.axis_index("ab")
        for ref, first, away, slab in (
            (own_ref, 0, 0, 0),
            (own_ref, 32, 0, 1),
            (near_ref, 0, 3, 0),
            (near_ref, 32, 1, 1),
            (far_ref, 0, 3, 1),
            (far_ref, 32, 1, 0),
            (total_ref, 0, 2, 0),
            (total_ref, 32, 2, 1),
        ):
            group = lax.rem(me + away, 4)
            for pair in range(16):
                out_ref[16 * group + pair, 2 * slab : 2 * slab + 2, :] = ref[first + 2 * pair : first + 2 * pair + 2, :]


def last_sums(pieces, slabs, weights, integrals, first_step, own, near, far, opposite):
    pairs, columns = pieces[0].shape[1], integrals.shape[1]
    whole = pl.BlockSpec((64, columns), lambda k: (0, 0))
    return pl.pallas_call(
        functools.partial(last_kernel, slabs),
        grid=(pairs // STEP,),
        in_specs=[pl.BlockSpec((piece.shape[0], STEP), lambda k: (0, k)) for piece in pieces]
        + [
            pl.BlockSpec((2, STEP), lambda k: (0, k + first_step)),
            pl.BlockSpec((STEP, columns), lambda k: (k + first_step, 0)),
        ]
        + [whole] * 4,
        out_specs=pl.BlockSpec((64, 4, columns), lambda k: (0, 0, 0)),
        out_shape=jax.ShapeDtypeStruct((64, 4, columns), F32),
        scratch_shapes=[pltpu.VMEM((64, columns), F32)],
        compiler_params=pltpu.CompilerParams(vmem_limit_bytes=40 * 2**20),
        cost_estimate=pl.CostEstimate(
            flops=6 * 64 * pairs * columns, bytes_accessed=4 * pairs * (64 + columns), transcendentals=0
        ),
    )(*pieces, weights, integrals, own, near, far, opposite)


def local(amplitudes, integrals, c_index, d_index, a_index, b_index):
    def right(x):
        return lax.ppermute(x, "ab", [(i, (i + 1) % 4) for i in range(4)])

    def left(x):
        return lax.ppermute(x, "ab", [(i, (i - 1) % 4) for i in range(4)])

    pairs, columns = integrals.shape
    half = pairs // 2
    plus, minus = amplitudes[0], amplitudes[1]
    right_plus, left_minus = right(plus), left(minus)
    right_minus, left_plus = right(minus), left(plus)
    onward = [right(right_plus[:, :half]), left(left_minus[:, :half])]
    onward_last = [right(right_plus[:, half:]), left(left_minus[:, half:])]

    same = c_index == d_index
    weights = jnp.stack([jnp.where(same, F32(0.5), F32(1.0)), jnp.where(same, F32(0.0), F32(1.0))])
    own = partial_sums([plus, minus], (0, 1), weights, integrals)
    near = partial_sums([right_plus, left_minus], (0, 1), weights, integrals)
    far = partial_sums([right_minus, left_plus], (1, 0), weights, integrals)
    opposite = partial_sums(onward, (0, 1), weights, integrals)
    part_sum = last_sums(onward_last, (0, 1), weights, integrals, half // STEP, own, near, far, opposite)

    shares = lax.all_to_all(part_sum, "cd", 0, 0, tiled=True)
    summed = jnp.sum(shares.reshape(64, 4, columns), axis=0).reshape(2, 2, columns).transpose(1, 0, 2)
    keep = jnp.where(a_index == b_index, F32(0.0), F32(1.0))
    factor = 0.5 * jnp.stack([jnp.ones_like(keep), keep])
    return summed * factor[None, :, :]


def solution(mesh):
    placed = (P(None, "ab", "cd"), P("cd", "ab"), P("cd"), P("cd"), P("ab"), P("ab"))
    return jax.shard_map(local, mesh=mesh, in_specs=placed, out_specs=P("cd", None, "ab"), check_vma=False)
```

```python
import functools

import jax
import jax.numpy as jnp
from jax import lax
from jax.experimental import pallas as pl
from jax.experimental.pallas import tpu as pltpu
from jax.sharding import PartitionSpec as P

F32 = jnp.float32
BF16 = jnp.bfloat16
STEP = 1792
VMEM = pltpu.CompilerParams(vmem_limit_bytes=24 * 2**20)
FREE = pl.CostEstimate(flops=0, bytes_accessed=0, transcendentals=0)
GROUPS, LAYERS, CORES = 4, 8, 2


def halves(x):
    high = x.astype(BF16)
    return high, (x - high.astype(F32)).astype(BF16)


def products(rows, block):
    count = rows.shape[0]
    high, low = halves(rows)
    block_high, block_low = halves(block)
    first = jnp.dot(jnp.concatenate([high, low], axis=0), block_high, preferred_element_type=F32)
    return first[:count] + (first[count:] + jnp.dot(high, block_low, preferred_element_type=F32))


def add_step(slabs, piece_refs, weight_ref, block_ref, total_ref):
    rows = [
        ref[...].reshape(-1, ref.shape[-1]) * weight_ref[slab : slab + 1, :] for ref, slab in zip(piece_refs, slabs)
    ]
    total_ref[...] += products(jnp.concatenate(rows, axis=0), block_ref[...])


def sum_kernel(slabs, *refs):
    n = len(slabs)
    total_ref = refs[n + 2]

    @pl.when(pl.program_id(0) == 0)
    def _():
        total_ref[...] = jnp.zeros_like(total_ref)

    add_step(slabs, refs[:n], refs[n], refs[n + 1], total_ref)


def specs(piece_specs, columns, first):
    return piece_specs + [
        pl.BlockSpec((2, STEP), lambda k: (0, k + first)),
        pl.BlockSpec((STEP, columns), lambda k: (k + first, 0)),
    ]


def own_sums(amplitudes, weights, integrals):
    slabs, rows, pairs = amplitudes.shape
    columns = integrals.shape[1]
    own = [pl.BlockSpec((1, rows, STEP), lambda k, s=s: (s, 0, k)) for s in range(slabs)]
    return pl.pallas_call(
        functools.partial(sum_kernel, (0, 1)),
        grid=(pairs // STEP,),
        in_specs=specs(own, columns, 0),
        out_specs=pl.BlockSpec((slabs * rows, columns), lambda k: (0, 0)),
        out_shape=jax.ShapeDtypeStruct((slabs * rows, columns), F32),
        compiler_params=VMEM,
        cost_estimate=FREE,
    )(amplitudes, amplitudes, weights, integrals)


def partial_sums(pieces, slabs, weights, integrals, first=0):
    n, (rows, pairs) = len(pieces), pieces[0].shape
    columns = integrals.shape[1]
    return pl.pallas_call(
        functools.partial(sum_kernel, slabs),
        grid=(pairs // STEP,),
        in_specs=specs([pl.BlockSpec((rows, STEP), lambda k: (0, k))] * n, columns, first),
        out_specs=pl.BlockSpec((n * rows, columns), lambda k: (0, 0)),
        out_shape=jax.ShapeDtypeStruct((n * rows, columns), F32),
        compiler_params=VMEM,
        cost_estimate=FREE,
    )(*pieces, weights, integrals)


def last_kernel(slabs, *refs):
    n = len(slabs)
    own_ref, near_ref, far_ref, opposite_ref, mine_ref, other_ref, total_ref = refs[n + 2 :]
    step = pl.program_id(0)

    @pl.when(step == 0)
    def _():
        total_ref[...] = opposite_ref[...]

    add_step(slabs, refs[:n], refs[n], refs[n + 1], total_ref)

    @pl.when(step == pl.num_programs(0) - 1)
    def _():
        me, core = lax.axis_index("ab"), lax.rem(lax.axis_index("cd"), CORES)
        for ref, start, away, slab in (
            (own_ref, 0, 0, 0),
            (own_ref, 32, 0, 1),
            (near_ref, 0, 3, 0),
            (near_ref, 32, 1, 1),
            (far_ref, 0, 3, 1),
            (far_ref, 32, 1, 0),
            (total_ref, 0, 2, 0),
            (total_ref, 32, 2, 1),
        ):
            group = lax.rem(me + away, GROUPS)
            for layer in range(LAYERS):
                pair = start + 2 * CORES * layer
                first, second = ref[pair : pair + 2, :], ref[pair + 2 : pair + 4, :]
                at = LAYERS * group + layer, slice(2 * slab, 2 * slab + 2)
                mine_ref[at] = jnp.where(core == 0, first, second)
                other_ref[at] = jnp.where(core == 0, second, first)


def last_sums(pieces, slabs, weights, integrals, first, own, near, far, opposite):
    n, (rows, pairs) = len(pieces), pieces[0].shape
    columns = integrals.shape[1]
    whole = [pl.BlockSpec(x.shape, lambda k: (0, 0)) for x in (own, near, far, opposite)]
    return pl.pallas_call(
        functools.partial(last_kernel, slabs),
        grid=(pairs // STEP,),
        in_specs=specs([pl.BlockSpec((rows, STEP), lambda k: (0, k))] * n, columns, first) + whole,
        out_specs=[pl.BlockSpec((GROUPS * LAYERS, 4, columns), lambda k: (0, 0, 0))] * 2,
        out_shape=[jax.ShapeDtypeStruct((GROUPS * LAYERS, 4, columns), F32)] * 2,
        scratch_shapes=[pltpu.VMEM((n * rows, columns), F32)],
        compiler_params=VMEM,
        cost_estimate=FREE,
    )(*pieces, weights, integrals, own, near, far, opposite)


def finish_kernel(shares_ref, a_ref, b_ref, out_ref):
    keep = jnp.where(a_ref[...] == b_ref[...], F32(0.0), F32(0.5))
    summed = jnp.sum(shares_ref[...], axis=0)
    out_ref[:, 0, :] = 0.5 * summed[0:2]
    out_ref[:, 1, :] = keep * summed[2:4]


def pieces_kernel(own_ref, *refs):
    plus_ref, minus_ref = refs[-2:]
    plus_ref[...] = own_ref[0]
    minus_ref[...] = own_ref[1]


def slabs_after(amplitudes, *after):
    _, rows, pairs = amplitudes.shape
    return pl.pallas_call(
        pieces_kernel,
        grid=(pairs // STEP,),
        in_specs=[pl.BlockSpec((2, rows, STEP), lambda k: (0, 0, k))] + [pl.BlockSpec(memory_space=pl.ANY)] * len(after),
        out_specs=[pl.BlockSpec((rows, STEP), lambda k: (0, k))] * 2,
        out_shape=[jax.ShapeDtypeStruct((rows, pairs), F32)] * 2,
        compiler_params=VMEM,
        cost_estimate=FREE,
    )(amplitudes, *after)


def right(x):
    return lax.ppermute(x, "ab", [(i, (i + 1) % GROUPS) for i in range(GROUPS)])


def left(x):
    return lax.ppermute(x, "ab", [(i, (i - 1) % GROUPS) for i in range(GROUPS)])


def over_cores(x):
    return lax.ppermute(x, "cd", [(i, i ^ 1) for i in range(GROUPS * LAYERS * CORES)])


def local(amplitudes, integrals, c_index, d_index, a_index, b_index):
    pairs, columns = integrals.shape
    cut = pairs // 4 * 3

    same = c_index == d_index
    weights = jnp.stack([jnp.where(same, F32(0.5), F32(1.0)), jnp.where(same, F32(0.0), F32(1.0))])

    right_plus, left_minus = right(amplitudes[0]), left(amplitudes[1])
    own = own_sums(amplitudes, weights, integrals)
    plus, minus = slabs_after(amplitudes, own)
    right_minus, left_plus = right(minus), left(plus)
    onward = [right(right_plus[:, :cut]), left(left_minus[:, :cut])]
    onward_last = [right(right_plus[:, cut:]), left(left_minus[:, cut:])]
    near = partial_sums([right_plus, left_minus], (0, 1), weights, integrals)
    far = partial_sums([right_minus, left_plus], (1, 0), weights, integrals)
    opposite = partial_sums(onward, (0, 1), weights, integrals)
    mine, other = last_sums(onward_last, (0, 1), weights, integrals, cut // STEP, own, near, far, opposite)

    both_cores = mine + over_cores(other)
    planes = [[2 * i + core for i in range(GROUPS * LAYERS)] for core in range(CORES)]
    shares = lax.all_to_all(both_cores, "cd", 0, 0, tiled=True, axis_index_groups=planes)
    return pl.pallas_call(
        finish_kernel, out_shape=jax.ShapeDtypeStruct((2, 2, columns), F32), compiler_params=VMEM, cost_estimate=FREE
    )(shares, a_index.reshape(1, columns), b_index.reshape(1, columns))


def solution(mesh):
    placed = (P(None, "ab", "cd"), P("cd", "ab"), P("cd"), P("cd"), P("ab"), P("ab"))
    return jax.shard_map(local, mesh=mesh, in_specs=placed, out_specs=P("cd", None, "ab"), check_vma=False)
```

```python
import functools

import jax
import jax.numpy as jnp
from jax import lax
from jax.experimental import pallas as pl
from jax.experimental.pallas import tpu as pltpu
from jax.sharding import PartitionSpec as P

F32 = jnp.float32
BF16 = jnp.bfloat16
STEP = 1792
VMEM = pltpu.CompilerParams(vmem_limit_bytes=24 * 2**20)
FREE = pl.CostEstimate(flops=0, bytes_accessed=0, transcendentals=0)
GROUPS, LAYERS, CORES = 4, 8, 2


def halves(x):
    high = x.astype(BF16)
    return high, (x - high.astype(F32)).astype(BF16)


def products(rows, block):
    count = rows.shape[0]
    high, low = halves(rows)
    block_high, block_low = halves(block)
    first = jnp.dot(jnp.concatenate([high, low], axis=0), block_high, preferred_element_type=F32)
    return first[:count] + (first[count:] + jnp.dot(high, block_low, preferred_element_type=F32))


def add_step(slabs, piece_refs, weight_ref, block_ref, total_ref):
    rows = [
        ref[...].reshape(-1, ref.shape[-1]) * weight_ref[slab : slab + 1, :] for ref, slab in zip(piece_refs, slabs)
    ]
    total_ref[...] += products(jnp.concatenate(rows, axis=0), block_ref[...])


def sum_kernel(slabs, *refs):
    n, total_ref = len(slabs), refs[-1]

    @pl.when(pl.program_id(0) == 0)
    def _():
        total_ref[...] = jnp.zeros_like(total_ref)

    add_step(slabs, refs[:n], refs[n], refs[n + 1], total_ref)


def specs(piece_specs, columns, first):
    return piece_specs + [
        pl.BlockSpec((2, STEP), lambda k: (0, k + first)),
        pl.BlockSpec((STEP, columns), lambda k: (k + first, 0)),
    ]


def own_sums(amplitudes, weights, integrals, after):
    slabs, rows, pairs = amplitudes.shape
    columns = integrals.shape[1]
    own = [pl.BlockSpec((1, rows, STEP), lambda k, s=s: (s, 0, k)) for s in range(slabs)]
    return pl.pallas_call(
        functools.partial(sum_kernel, (0, 1)),
        grid=(pairs // STEP,),
        in_specs=specs(own, columns, 0) + [pl.BlockSpec(memory_space=pl.ANY)] * len(after),
        out_specs=pl.BlockSpec((slabs * rows, columns), lambda k: (0, 0)),
        out_shape=jax.ShapeDtypeStruct((slabs * rows, columns), F32),
        compiler_params=VMEM,
        cost_estimate=FREE,
    )(amplitudes, amplitudes, weights, integrals, *after)


def partial_sums(pieces, slabs, weights, integrals, first=0, after=()):
    n, (rows, pairs) = len(pieces), pieces[0].shape
    columns = integrals.shape[1]
    return pl.pallas_call(
        functools.partial(sum_kernel, slabs),
        grid=(pairs // STEP,),
        in_specs=specs([pl.BlockSpec((rows, STEP), lambda k: (0, k))] * n, columns, first)
        + [pl.BlockSpec(memory_space=pl.ANY)] * len(after),
        out_specs=pl.BlockSpec((n * rows, columns), lambda k: (0, 0)),
        out_shape=jax.ShapeDtypeStruct((n * rows, columns), F32),
        compiler_params=VMEM,
        cost_estimate=FREE,
    )(*pieces, weights, integrals, *after)


def lay_out(ref, start, slab, group, core, mine_ref, other_ref):
    for layer in range(LAYERS):
        pair = start + 2 * CORES * layer
        first, second = ref[pair : pair + 2, :], ref[pair + 2 : pair + 4, :]
        at = LAYERS * group + layer, slice(2 * slab, 2 * slab + 2)
        mine_ref[at] = jnp.where(core == 0, first, second)
        other_ref[at] = jnp.where(core == 0, second, first)


def exchange_kernel(own_ref, near_ref, far_ref, mine_ref, other_ref):
    me, core = lax.axis_index("ab"), lax.rem(lax.axis_index("cd"), CORES)
    opposite = pl.ds(LAYERS * lax.rem(me + 2, GROUPS), LAYERS)
    mine_ref[opposite] = jnp.zeros((LAYERS, *mine_ref.shape[1:]), F32)
    other_ref[opposite] = jnp.zeros((LAYERS, *mine_ref.shape[1:]), F32)
    for ref, start, away, slab in (
        (own_ref, 0, 0, 0),
        (own_ref, 32, 0, 1),
        (near_ref, 0, 3, 0),
        (near_ref, 32, 1, 1),
        (far_ref, 0, 3, 1),
        (far_ref, 32, 1, 0),
    ):
        lay_out(ref, start, slab, lax.rem(me + away, GROUPS), core, mine_ref, other_ref)


def exchange(own, near, far):
    shape = (GROUPS * LAYERS, 4, own.shape[1])
    return pl.pallas_call(
        exchange_kernel,
        out_shape=[jax.ShapeDtypeStruct(shape, F32)] * 2,
        compiler_params=VMEM,
        cost_estimate=FREE,
    )(own, near, far)


def opposite_kernel(slabs, *refs):
    n = len(slabs)
    before_ref, mine_ref, other_ref, total_ref = refs[n + 2 :]
    step = pl.program_id(0)

    @pl.when(step == 0)
    def _():
        total_ref[...] = before_ref[...]

    add_step(slabs, refs[:n], refs[n], refs[n + 1], total_ref)

    @pl.when(step == pl.num_programs(0) - 1)
    def _():
        core = lax.rem(lax.axis_index("cd"), CORES)
        for slab in range(2):
            lay_out(total_ref, 32 * slab, slab, 0, core, mine_ref, other_ref)


def opposite_sums(pieces, slabs, weights, integrals, first, before):
    n, (rows, pairs) = len(pieces), pieces[0].shape
    columns = integrals.shape[1]
    return pl.pallas_call(
        functools.partial(opposite_kernel, slabs),
        grid=(pairs // STEP,),
        in_specs=specs([pl.BlockSpec((rows, STEP), lambda k: (0, k))] * n, columns, first)
        + [pl.BlockSpec(before.shape, lambda k: (0, 0))],
        out_specs=[pl.BlockSpec((LAYERS, 4, columns), lambda k: (0, 0, 0))] * 2,
        out_shape=[jax.ShapeDtypeStruct((LAYERS, 4, columns), F32)] * 2,
        scratch_shapes=[pltpu.VMEM((n * rows, columns), F32)],
        compiler_params=VMEM,
        cost_estimate=FREE,
    )(*pieces, weights, integrals, before)


def last_kernel(mine_ref, got_ref, mine_opposite_ref, got_opposite_ref, out_ref):
    group = lax.rem(lax.axis_index("ab") + 2, GROUPS)
    out_ref[...] = mine_ref[...] + got_ref[...]
    out_ref[pl.ds(LAYERS * group, LAYERS)] = mine_opposite_ref[...] + got_opposite_ref[...]


def last_sums(*arrays):
    return pl.pallas_call(
        last_kernel,
        out_shape=jax.ShapeDtypeStruct(arrays[0].shape, F32),
        compiler_params=VMEM,
        cost_estimate=FREE,
    )(*arrays)


def finish_kernel(shares_ref, a_ref, b_ref, out_ref):
    keep = jnp.where(a_ref[...] == b_ref[...], F32(0.0), F32(0.5))
    summed = jnp.sum(shares_ref[...], axis=0)
    out_ref[:, 0, :] = 0.5 * summed[0:2]
    out_ref[:, 1, :] = keep * summed[2:4]


def pieces_kernel(own_ref, *refs):
    plus_ref, minus_ref = refs[-2:]
    plus_ref[...] = own_ref[0]
    minus_ref[...] = own_ref[1]


def slabs_after(amplitudes, pairs, *after):
    rows = amplitudes.shape[1]
    return pl.pallas_call(
        pieces_kernel,
        grid=(pairs // STEP,),
        in_specs=[pl.BlockSpec((2, rows, STEP), lambda k: (0, 0, k))] + [pl.BlockSpec(memory_space=pl.ANY)] * len(after),
        out_specs=[pl.BlockSpec((rows, STEP), lambda k: (0, k))] * 2,
        out_shape=[jax.ShapeDtypeStruct((rows, pairs), F32)] * 2,
        compiler_params=VMEM,
        cost_estimate=FREE,
    )(amplitudes, *after)


def right(x):
    return lax.ppermute(x, "ab", [(i, (i + 1) % GROUPS) for i in range(GROUPS)])


def left(x):
    return lax.ppermute(x, "ab", [(i, (i - 1) % GROUPS) for i in range(GROUPS)])


def over_cores(x):
    return lax.ppermute(x, "cd", [(i, i ^ 1) for i in range(GROUPS * LAYERS * CORES)])


def local(amplitudes, integrals, c_index, d_index, a_index, b_index):
    pairs, columns = integrals.shape
    cut = pairs - STEP

    same = c_index == d_index
    weights = jnp.stack([jnp.where(same, F32(0.5), F32(1.0)), jnp.where(same, F32(0.0), F32(1.0))])

    right_last, left_last = right(amplitudes[0, :, cut:]), left(amplitudes[1, :, cut:])
    plus, minus = slabs_after(amplitudes, cut)
    right_plus, left_minus = right(plus), left(minus)
    own = own_sums(amplitudes, weights, integrals, (right_last, left_last))
    plus, minus = slabs_after(amplitudes, pairs, own)
    right_minus, left_plus = right(minus), left(plus)
    onward = [right(right_plus), left(left_minus)]
    onward_last = [right(right_last), left(left_last)]

    near = partial_sums([right_plus, left_minus], (0, 1), weights, integrals)
    near = partial_sums([right_last, left_last], (0, 1), weights, integrals, cut // STEP) + near
    far = partial_sums([right_minus, left_plus], (1, 0), weights, integrals)
    mine, other = exchange(own, near, far)
    got = over_cores(other)
    opposite = partial_sums(onward, (0, 1), weights, integrals, 0, (got,))
    mine_opposite, other = opposite_sums(onward_last, (0, 1), weights, integrals, cut // STEP, opposite)
    part_sum = last_sums(mine, got, mine_opposite, over_cores(other))

    planes = [[2 * i + core for i in range(GROUPS * LAYERS)] for core in range(CORES)]
    shares = lax.all_to_all(part_sum, "cd", 0, 0, tiled=True, axis_index_groups=planes)
    return pl.pallas_call(
        finish_kernel, out_shape=jax.ShapeDtypeStruct((2, 2, columns), F32), compiler_params=VMEM, cost_estimate=FREE
    )(shares, a_index.reshape(1, columns), b_index.reshape(1, columns))


def solution(mesh):
    placed = (P(None, "ab", "cd"), P("cd", "ab"), P("cd"), P("cd"), P("ab"), P("ab"))
    return jax.shard_map(local, mesh=mesh, in_specs=placed, out_specs=P("cd", None, "ab"), check_vma=False)
```

```python
import functools

import jax
import jax.numpy as jnp
from jax import lax
from jax.experimental import pallas as pl
from jax.experimental.pallas import tpu as pltpu
from jax.sharding import PartitionSpec as P

F32 = jnp.float32
BF16 = jnp.bfloat16
STEP = 1792
VMEM = pltpu.CompilerParams(vmem_limit_bytes=24 * 2**20)
FREE = pl.CostEstimate(flops=0, bytes_accessed=0, transcendentals=0)
GROUPS, LAYERS, CORES = 4, 8, 2
ORDER = (4, 5, 6, 7, 0, 1, 2, 3)


def halves(x):
    high = x.astype(BF16)
    return high, (x - high.astype(F32)).astype(BF16)


def products(rows, block):
    count = rows.shape[0]
    high, low = halves(rows)
    block_high, block_low = halves(block)
    first = jnp.dot(jnp.concatenate([high, low], axis=0), block_high, preferred_element_type=F32)
    return first[:count] + (first[count:] + jnp.dot(high, block_low, preferred_element_type=F32))


def add_step(slabs, piece_refs, weight_ref, block_ref, total_ref):
    rows = [
        ref[...].reshape(-1, ref.shape[-1]) * weight_ref[slab : slab + 1, :] for ref, slab in zip(piece_refs, slabs)
    ]
    total_ref[...] += products(jnp.concatenate(rows, axis=0), block_ref[...])


def sum_kernel(slabs, *refs):
    n, total_ref = len(slabs), refs[-1]

    @pl.when(pl.program_id(0) == 0)
    def _():
        total_ref[...] = jnp.zeros_like(total_ref)

    add_step(slabs, refs[:n], refs[n], refs[n + 1], total_ref)


def specs(piece_specs, columns, first):
    return piece_specs + [
        pl.BlockSpec((2, STEP), lambda k: (0, k + first)),
        pl.BlockSpec((STEP, columns), lambda k: (k + first, 0)),
    ]


def own_sums(amplitudes, weights, integrals, after):
    slabs, rows, pairs = amplitudes.shape
    columns = integrals.shape[1]
    own = [pl.BlockSpec((1, rows, STEP), lambda k, s=s: (s, 0, k)) for s in range(slabs)]
    return pl.pallas_call(
        functools.partial(sum_kernel, (0, 1)),
        grid=(pairs // STEP,),
        in_specs=specs(own, columns, 0) + [pl.BlockSpec(memory_space=pl.ANY)] * len(after),
        out_specs=pl.BlockSpec((slabs * rows, columns), lambda k: (0, 0)),
        out_shape=jax.ShapeDtypeStruct((slabs * rows, columns), F32),
        compiler_params=VMEM,
        cost_estimate=FREE,
    )(amplitudes, amplitudes, weights, integrals, *after)


def partial_sums(pieces, slabs, weights, integrals, first=0, after=()):
    n, (rows, pairs) = len(pieces), pieces[0].shape
    columns = integrals.shape[1]
    return pl.pallas_call(
        functools.partial(sum_kernel, slabs),
        grid=(pairs // STEP,),
        in_specs=specs([pl.BlockSpec((rows, STEP), lambda k: (0, k))] * n, columns, first)
        + [pl.BlockSpec(memory_space=pl.ANY)] * len(after),
        out_specs=pl.BlockSpec((n * rows, columns), lambda k: (0, 0)),
        out_shape=jax.ShapeDtypeStruct((n * rows, columns), F32),
        compiler_params=VMEM,
        cost_estimate=FREE,
    )(*pieces, weights, integrals, *after)


def place(layer, group):
    return GROUPS * ORDER.index(layer) + GROUPS - 1 - group


def lay_out(ref, start, slab, at, core, mine_ref, other_ref):
    for layer in range(LAYERS):
        pair = start + 2 * CORES * layer
        first, second = ref[pair : pair + 2, :], ref[pair + 2 : pair + 4, :]
        half = slice(2 * slab, 2 * slab + 2)
        mine_ref[at(layer), half] = jnp.where(core == 0, first, second)
        other_ref[at(layer), half] = jnp.where(core == 0, second, first)


def exchange_kernel(own_ref, near_ref, far_ref, mine_ref, other_ref):
    me, core = lax.axis_index("ab"), lax.rem(lax.axis_index("cd"), CORES)
    for layer in range(LAYERS):
        opposite = place(layer, lax.rem(me + 2, GROUPS))
        mine_ref[opposite] = jnp.zeros(mine_ref.shape[1:], F32)
        other_ref[opposite] = jnp.zeros(mine_ref.shape[1:], F32)
    for ref, start, away, slab in (
        (own_ref, 0, 0, 0),
        (own_ref, 32, 0, 1),
        (near_ref, 0, 3, 0),
        (near_ref, 32, 1, 1),
        (far_ref, 0, 3, 1),
        (far_ref, 32, 1, 0),
    ):
        group = lax.rem(me + away, GROUPS)
        lay_out(ref, start, slab, functools.partial(place, group=group), core, mine_ref, other_ref)


def exchange(own, near, far):
    shape = (GROUPS * LAYERS, 4, own.shape[1])
    return pl.pallas_call(
        exchange_kernel,
        out_shape=[jax.ShapeDtypeStruct(shape, F32)] * 2,
        compiler_params=VMEM,
        cost_estimate=FREE,
    )(own, near, far)


def opposite_kernel(slabs, *refs):
    n = len(slabs)
    before_ref, mine_ref, other_ref, total_ref = refs[n + 2 :]
    step = pl.program_id(0)

    @pl.when(step == 0)
    def _():
        total_ref[...] = before_ref[...]

    add_step(slabs, refs[:n], refs[n], refs[n + 1], total_ref)

    @pl.when(step == pl.num_programs(0) - 1)
    def _():
        core = lax.rem(lax.axis_index("cd"), CORES)
        for slab in range(2):
            lay_out(total_ref, 32 * slab, slab, lambda layer: layer, core, mine_ref, other_ref)


def opposite_sums(pieces, slabs, weights, integrals, first, before):
    n, (rows, pairs) = len(pieces), pieces[0].shape
    columns = integrals.shape[1]
    return pl.pallas_call(
        functools.partial(opposite_kernel, slabs),
        grid=(pairs // STEP,),
        in_specs=specs([pl.BlockSpec((rows, STEP), lambda k: (0, k))] * n, columns, first)
        + [pl.BlockSpec(before.shape, lambda k: (0, 0))],
        out_specs=[pl.BlockSpec((LAYERS, 4, columns), lambda k: (0, 0, 0))] * 2,
        out_shape=[jax.ShapeDtypeStruct((LAYERS, 4, columns), F32)] * 2,
        scratch_shapes=[pltpu.VMEM((n * rows, columns), F32)],
        compiler_params=VMEM,
        cost_estimate=FREE,
    )(*pieces, weights, integrals, before)


def last_kernel(mine_ref, got_ref, mine_opposite_ref, got_opposite_ref, out_ref):
    group = lax.rem(lax.axis_index("ab") + 2, GROUPS)
    out_ref[...] = mine_ref[...] + got_ref[...]
    for layer in range(LAYERS):
        out_ref[place(layer, group)] = mine_opposite_ref[layer] + got_opposite_ref[layer]


def last_sums(*arrays):
    return pl.pallas_call(
        last_kernel,
        out_shape=jax.ShapeDtypeStruct(arrays[0].shape, F32),
        compiler_params=VMEM,
        cost_estimate=FREE,
    )(*arrays)


def finish_kernel(shares_ref, a_ref, b_ref, out_ref):
    keep = jnp.where(a_ref[...] == b_ref[...], F32(0.0), F32(0.5))
    summed = jnp.sum(shares_ref[...], axis=0)
    out_ref[:, 0, :] = 0.5 * summed[0:2]
    out_ref[:, 1, :] = keep * summed[2:4]


def pieces_kernel(own_ref, *refs):
    plus_ref, minus_ref = refs[-2:]
    plus_ref[...] = own_ref[0]
    minus_ref[...] = own_ref[1]


def slabs_after(amplitudes, pairs, *after):
    rows = amplitudes.shape[1]
    return pl.pallas_call(
        pieces_kernel,
        grid=(pairs // STEP,),
        in_specs=[pl.BlockSpec((2, rows, STEP), lambda k: (0, 0, k))] + [pl.BlockSpec(memory_space=pl.ANY)] * len(after),
        out_specs=[pl.BlockSpec((rows, STEP), lambda k: (0, k))] * 2,
        out_shape=[jax.ShapeDtypeStruct((rows, pairs), F32)] * 2,
        compiler_params=VMEM,
        cost_estimate=FREE,
    )(amplitudes, *after)


def right(x):
    return lax.ppermute(x, "ab", [(i, (i + 1) % GROUPS) for i in range(GROUPS)])


def left(x):
    return lax.ppermute(x, "ab", [(i, (i - 1) % GROUPS) for i in range(GROUPS)])


def over_cores(x):
    return lax.ppermute(x, "cd", [(i, i ^ 1) for i in range(GROUPS * LAYERS * CORES)])


def local(amplitudes, integrals, c_index, d_index, a_index, b_index):
    pairs, columns = integrals.shape
    cut = pairs - STEP

    same = c_index == d_index
    weights = jnp.stack([jnp.where(same, F32(0.5), F32(1.0)), jnp.where(same, F32(0.0), F32(1.0))])

    right_last, left_last = right(amplitudes[0, :, cut:]), left(amplitudes[1, :, cut:])
    plus, minus = slabs_after(amplitudes, cut)
    right_plus, left_minus = right(plus), left(minus)
    own = own_sums(amplitudes, weights, integrals, (right_last, left_last))
    plus, minus = slabs_after(amplitudes, pairs, own)
    right_minus, left_plus = right(minus), left(plus)
    onward = [right(right_plus), left(left_minus)]
    onward_last = [right(right_last), left(left_last)]

    near = partial_sums([right_plus, left_minus], (0, 1), weights, integrals)
    near = partial_sums([right_last, left_last], (0, 1), weights, integrals, cut // STEP) + near
    far = partial_sums([right_minus, left_plus], (1, 0), weights, integrals)
    mine, other = exchange(own, near, far)
    got = over_cores(other)
    opposite = partial_sums(onward, (0, 1), weights, integrals, 0, (got,))
    mine_opposite, other = opposite_sums(onward_last, (0, 1), weights, integrals, cut // STEP, opposite)
    part_sum = last_sums(mine, got, mine_opposite, over_cores(other))

    planes = [
        [CORES * (LAYERS * group + layer) + core for layer in ORDER for group in reversed(range(GROUPS))] for core in range(CORES)
    ]
    shares = lax.all_to_all(part_sum, "cd", 0, 0, tiled=True, axis_index_groups=planes)
    return pl.pallas_call(
        finish_kernel, out_shape=jax.ShapeDtypeStruct((2, 2, columns), F32), compiler_params=VMEM, cost_estimate=FREE
    )(shares, a_index.reshape(1, columns), b_index.reshape(1, columns))


def solution(mesh):
    placed = (P(None, "ab", "cd"), P("cd", "ab"), P("cd"), P("cd"), P("ab"), P("ab"))
    return jax.shard_map(local, mesh=mesh, in_specs=placed, out_specs=P("cd", None, "ab"), check_vma=False)
```

```python
import functools

import jax
import jax.numpy as jnp
from jax import lax
from jax.experimental import pallas as pl
from jax.experimental.pallas import tpu as pltpu
from jax.sharding import PartitionSpec as P

F32 = jnp.float32
BF16 = jnp.bfloat16
STEP = 1792
TAIL = 896
VMEM = pltpu.CompilerParams(vmem_limit_bytes=24 * 2**20)
FREE = pl.CostEstimate(flops=0, bytes_accessed=0, transcendentals=0)
GROUPS, LAYERS, CORES = 4, 8, 2
ORDER = (4, 5, 6, 7, 0, 1, 2, 3)


def halves(x):
    high = x.astype(BF16)
    return high, (x - high.astype(F32)).astype(BF16)


def products(rows, block):
    count = rows.shape[0]
    high, low = halves(rows)
    block_high, block_low = halves(block)
    first = jnp.dot(jnp.concatenate([high, low], axis=0), block_high, preferred_element_type=F32)
    return first[:count] + (first[count:] + jnp.dot(high, block_low, preferred_element_type=F32))


def add_step(slabs, piece_refs, weight_ref, block_ref, total_ref):
    rows = [
        ref[...].reshape(-1, ref.shape[-1]) * weight_ref[slab : slab + 1, :] for ref, slab in zip(piece_refs, slabs)
    ]
    total_ref[...] += products(jnp.concatenate(rows, axis=0), block_ref[...])


def sum_kernel(slabs, *refs):
    n, total_ref = len(slabs), refs[-1]

    @pl.when(pl.program_id(0) == 0)
    def _():
        total_ref[...] = jnp.zeros_like(total_ref)

    add_step(slabs, refs[:n], refs[n], refs[n + 1], total_ref)


def specs(piece_specs, columns, first, step=STEP):
    return piece_specs + [
        pl.BlockSpec((2, step), lambda k: (0, k + first)),
        pl.BlockSpec((step, columns), lambda k: (k + first, 0)),
    ]


def own_sums(amplitudes, weights, integrals, after):
    slabs, rows, pairs = amplitudes.shape
    columns = integrals.shape[1]
    own = [pl.BlockSpec((1, rows, STEP), lambda k, s=s: (s, 0, k)) for s in range(slabs)]
    return pl.pallas_call(
        functools.partial(sum_kernel, (0, 1)),
        grid=(pairs // STEP,),
        in_specs=specs(own, columns, 0) + [pl.BlockSpec(memory_space=pl.ANY)] * len(after),
        out_specs=pl.BlockSpec((slabs * rows, columns), lambda k: (0, 0)),
        out_shape=jax.ShapeDtypeStruct((slabs * rows, columns), F32),
        compiler_params=VMEM,
        cost_estimate=FREE,
    )(amplitudes, amplitudes, weights, integrals, *after)


def partial_sums(pieces, slabs, weights, integrals, first=0, after=()):
    n, (rows, pairs) = len(pieces), pieces[0].shape
    columns = integrals.shape[1]
    return pl.pallas_call(
        functools.partial(sum_kernel, slabs),
        grid=(pairs // STEP,),
        in_specs=specs([pl.BlockSpec((rows, STEP), lambda k: (0, k))] * n, columns, first)
        + [pl.BlockSpec(memory_space=pl.ANY)] * len(after),
        out_specs=pl.BlockSpec((n * rows, columns), lambda k: (0, 0)),
        out_shape=jax.ShapeDtypeStruct((n * rows, columns), F32),
        compiler_params=VMEM,
        cost_estimate=FREE,
    )(*pieces, weights, integrals, *after)


def place(layer, group):
    return GROUPS * ORDER.index(layer) + GROUPS - 1 - group


def lay_out(ref, start, slab, at, core, mine_ref, other_ref):
    for layer in range(LAYERS):
        pair = start + 2 * CORES * layer
        first, second = ref[pair : pair + 2, :], ref[pair + 2 : pair + 4, :]
        half = slice(2 * slab, 2 * slab + 2)
        mine_ref[at(layer), half] = jnp.where(core == 0, first, second)
        other_ref[at(layer), half] = jnp.where(core == 0, second, first)


def exchange_kernel(own_ref, near_ref, far_ref, mine_ref, other_ref):
    me, core = lax.axis_index("ab"), lax.rem(lax.axis_index("cd"), CORES)
    for layer in range(LAYERS):
        opposite = place(layer, lax.rem(me + 2, GROUPS))
        mine_ref[opposite] = jnp.zeros(mine_ref.shape[1:], F32)
        other_ref[opposite] = jnp.zeros(mine_ref.shape[1:], F32)
    for ref, start, away, slab in (
        (own_ref, 0, 0, 0),
        (own_ref, 32, 0, 1),
        (near_ref, 0, 3, 0),
        (near_ref, 32, 1, 1),
        (far_ref, 0, 3, 1),
        (far_ref, 32, 1, 0),
    ):
        group = lax.rem(me + away, GROUPS)
        lay_out(ref, start, slab, functools.partial(place, group=group), core, mine_ref, other_ref)


def exchange(own, near, far):
    shape = (GROUPS * LAYERS, 4, own.shape[1])
    return pl.pallas_call(
        exchange_kernel,
        out_shape=[jax.ShapeDtypeStruct(shape, F32)] * 2,
        compiler_params=VMEM,
        cost_estimate=FREE,
    )(own, near, far)


def opposite_kernel(slabs, *refs):
    n = len(slabs)
    before_ref, mine_ref, other_ref, total_ref = refs[n + 2 :]
    step = pl.program_id(0)

    @pl.when(step == 0)
    def _():
        total_ref[...] = before_ref[...]

    add_step(slabs, refs[:n], refs[n], refs[n + 1], total_ref)

    @pl.when(step == pl.num_programs(0) - 1)
    def _():
        core = lax.rem(lax.axis_index("cd"), CORES)
        for slab in range(2):
            lay_out(total_ref, 32 * slab, slab, lambda layer: layer, core, mine_ref, other_ref)


def opposite_sums(pieces, slabs, weights, integrals, first, before):
    n, (rows, pairs) = len(pieces), pieces[0].shape
    columns = integrals.shape[1]
    return pl.pallas_call(
        functools.partial(opposite_kernel, slabs),
        grid=(pairs // TAIL,),
        in_specs=specs([pl.BlockSpec((rows, TAIL), lambda k: (0, k))] * n, columns, first, TAIL)
        + [pl.BlockSpec(before.shape, lambda k: (0, 0))],
        out_specs=[pl.BlockSpec((LAYERS, 4, columns), lambda k: (0, 0, 0))] * 2,
        out_shape=[jax.ShapeDtypeStruct((LAYERS, 4, columns), F32)] * 2,
        scratch_shapes=[pltpu.VMEM((n * rows, columns), F32)],
        compiler_params=VMEM,
        cost_estimate=FREE,
    )(*pieces, weights, integrals, before)


def last_kernel(mine_ref, got_ref, mine_opposite_ref, got_opposite_ref, out_ref):
    group = lax.rem(lax.axis_index("ab") + 2, GROUPS)
    out_ref[...] = mine_ref[...] + got_ref[...]
    for layer in range(LAYERS):
        out_ref[place(layer, group)] = mine_opposite_ref[layer] + got_opposite_ref[layer]


def last_sums(*arrays):
    return pl.pallas_call(
        last_kernel,
        out_shape=jax.ShapeDtypeStruct(arrays[0].shape, F32),
        compiler_params=VMEM,
        cost_estimate=FREE,
    )(*arrays)


def finish_kernel(shares_ref, a_ref, b_ref, out_ref):
    keep = jnp.where(a_ref[...] == b_ref[...], F32(0.0), F32(0.5))
    summed = jnp.sum(shares_ref[...], axis=0)
    out_ref[:, 0, :] = 0.5 * summed[0:2]
    out_ref[:, 1, :] = keep * summed[2:4]


def pieces_kernel(own_ref, *refs):
    plus_ref, minus_ref = refs[-2:]
    plus_ref[...] = own_ref[0]
    minus_ref[...] = own_ref[1]


def slabs_after(amplitudes, pairs, *after):
    rows = amplitudes.shape[1]
    return pl.pallas_call(
        pieces_kernel,
        grid=(pairs // STEP,),
        in_specs=[pl.BlockSpec((2, rows, STEP), lambda k: (0, 0, k))] + [pl.BlockSpec(memory_space=pl.ANY)] * len(after),
        out_specs=[pl.BlockSpec((rows, STEP), lambda k: (0, k))] * 2,
        out_shape=[jax.ShapeDtypeStruct((rows, pairs), F32)] * 2,
        compiler_params=VMEM,
        cost_estimate=FREE,
    )(amplitudes, *after)


def right(x):
    return lax.ppermute(x, "ab", [(i, (i + 1) % GROUPS) for i in range(GROUPS)])


def left(x):
    return lax.ppermute(x, "ab", [(i, (i - 1) % GROUPS) for i in range(GROUPS)])


def over_cores(x):
    return lax.ppermute(x, "cd", [(i, i ^ 1) for i in range(GROUPS * LAYERS * CORES)])


def local(amplitudes, integrals, c_index, d_index, a_index, b_index):
    pairs, columns = integrals.shape
    cut = pairs - STEP

    same = c_index == d_index
    weights = jnp.stack([jnp.where(same, F32(0.5), F32(1.0)), jnp.where(same, F32(0.0), F32(1.0))])

    right_last, left_last = right(amplitudes[0, :, cut:]), left(amplitudes[1, :, cut:])
    plus, minus = slabs_after(amplitudes, cut)
    right_plus, left_minus = right(plus), left(minus)
    own = own_sums(amplitudes, weights, integrals, (right_last, left_last))
    plus, minus = slabs_after(amplitudes, pairs, own)
    right_minus, left_plus = right(minus), left(plus)
    onward = [right(right_plus), left(left_minus)]
    onward_last = [right(right_last), left(left_last)]

    near = partial_sums([right_plus, left_minus], (0, 1), weights, integrals)
    near = partial_sums([right_last, left_last], (0, 1), weights, integrals, cut // STEP) + near
    far = partial_sums([right_minus, left_plus], (1, 0), weights, integrals)
    mine, other = exchange(own, near, far)
    got = over_cores(other)
    opposite = partial_sums(onward, (0, 1), weights, integrals, 0, (got,))
    mine_opposite, other = opposite_sums(onward_last, (0, 1), weights, integrals, cut // TAIL, opposite)
    part_sum = last_sums(mine, got, mine_opposite, over_cores(other))

    planes = [
        [CORES * (LAYERS * group + layer) + core for layer in ORDER for group in reversed(range(GROUPS))] for core in range(CORES)
    ]
    shares = lax.all_to_all(part_sum, "cd", 0, 0, tiled=True, axis_index_groups=planes)
    return pl.pallas_call(
        finish_kernel, out_shape=jax.ShapeDtypeStruct((2, 2, columns), F32), compiler_params=VMEM, cost_estimate=FREE
    )(shares, a_index.reshape(1, columns), b_index.reshape(1, columns))


def solution(mesh):
    placed = (P(None, "ab", "cd"), P("cd", "ab"), P("cd"), P("cd"), P("ab"), P("ab"))
    return jax.shard_map(local, mesh=mesh, in_specs=placed, out_specs=P("cd", None, "ab"), check_vma=False)
```

```python
import functools

import jax
import jax.numpy as jnp
from jax import lax
from jax.experimental import pallas as pl
from jax.experimental.pallas import tpu as pltpu
from jax.sharding import PartitionSpec as P

F32 = jnp.float32
BF16 = jnp.bfloat16
STEP = 1792
VMEM = pltpu.CompilerParams(vmem_limit_bytes=32 * 2**20)
FREE = pl.CostEstimate(flops=0, bytes_accessed=0, transcendentals=0)
GROUPS, LAYERS, CORES = 4, 8, 2
ORDER = (4, 5, 6, 7, 0, 1, 2, 3)


def halves(x):
    high = x.astype(BF16)
    return high, (x - high.astype(F32)).astype(BF16)


def products(rows, block):
    count = rows.shape[0]
    high, low = halves(rows)
    block_high, block_low = halves(block)
    first = jnp.dot(jnp.concatenate([high, low], axis=0), block_high, preferred_element_type=F32)
    return first[:count] + (first[count:] + jnp.dot(high, block_low, preferred_element_type=F32))


def add_step(slabs, piece_refs, weight_ref, block_ref, total_ref):
    rows = [
        ref[...].reshape(-1, ref.shape[-1]) * weight_ref[slab : slab + 1, :] for ref, slab in zip(piece_refs, slabs)
    ]
    total_ref[...] += products(jnp.concatenate(rows, axis=0), block_ref[...])


def sum_kernel(slabs, *refs):
    n, total_ref = len(slabs), refs[-1]

    @pl.when(pl.program_id(0) == 0)
    def _():
        total_ref[...] = jnp.zeros_like(total_ref)

    add_step(slabs, refs[:n], refs[n], refs[n + 1], total_ref)


def specs(piece_specs, columns, first):
    return piece_specs + [
        pl.BlockSpec((2, STEP), lambda k: (0, k + first)),
        pl.BlockSpec((STEP, columns), lambda k: (k + first, 0)),
    ]


def own_sums(amplitudes, weights, integrals, after):
    slabs, rows, pairs = amplitudes.shape
    columns = integrals.shape[1]
    own = [pl.BlockSpec((1, rows, STEP), lambda k, s=s: (s, 0, k)) for s in range(slabs)]
    return pl.pallas_call(
        functools.partial(sum_kernel, (0, 1)),
        grid=(pairs // STEP,),
        in_specs=specs(own, columns, 0) + [pl.BlockSpec(memory_space=pl.ANY)] * len(after),
        out_specs=pl.BlockSpec((slabs * rows, columns), lambda k: (0, 0)),
        out_shape=jax.ShapeDtypeStruct((slabs * rows, columns), F32),
        compiler_params=VMEM,
        cost_estimate=FREE,
    )(amplitudes, amplitudes, weights, integrals, *after)


def partial_sums(pieces, slabs, weights, integrals, first=0, after=()):
    n, (rows, pairs) = len(pieces), pieces[0].shape
    columns = integrals.shape[1]
    return pl.pallas_call(
        functools.partial(sum_kernel, slabs),
        grid=(pairs // STEP,),
        in_specs=specs([pl.BlockSpec((rows, STEP), lambda k: (0, k))] * n, columns, first)
        + [pl.BlockSpec(memory_space=pl.ANY)] * len(after),
        out_specs=pl.BlockSpec((n * rows, columns), lambda k: (0, 0)),
        out_shape=jax.ShapeDtypeStruct((n * rows, columns), F32),
        compiler_params=VMEM,
        cost_estimate=FREE,
    )(*pieces, weights, integrals, *after)


def place(layer, group):
    return GROUPS * ORDER.index(layer) + GROUPS - 1 - group


def lay_out(ref, start, slab, at, core, mine_ref, other_ref):
    for layer in range(LAYERS):
        pair = start + 2 * CORES * layer
        first, second = ref[pair : pair + 2, :], ref[pair + 2 : pair + 4, :]
        half = slice(2 * slab, 2 * slab + 2)
        mine_ref[at(layer), half] = jnp.where(core == 0, first, second)
        other_ref[at(layer), half] = jnp.where(core == 0, second, first)


def exchange_kernel(own_ref, near_ref, far_ref, mine_ref, other_ref):
    me, core = lax.axis_index("ab"), lax.rem(lax.axis_index("cd"), CORES)
    for layer in range(LAYERS):
        opposite = place(layer, lax.rem(me + 2, GROUPS))
        mine_ref[opposite] = jnp.zeros(mine_ref.shape[1:], F32)
        other_ref[opposite] = jnp.zeros(mine_ref.shape[1:], F32)
    for ref, start, away, slab in (
        (own_ref, 0, 0, 0),
        (own_ref, 32, 0, 1),
        (near_ref, 0, 3, 0),
        (near_ref, 32, 1, 1),
        (far_ref, 0, 3, 1),
        (far_ref, 32, 1, 0),
    ):
        group = lax.rem(me + away, GROUPS)
        lay_out(ref, start, slab, functools.partial(place, group=group), core, mine_ref, other_ref)


def exchange(own, near, far):
    shape = (GROUPS * LAYERS, 4, own.shape[1])
    return pl.pallas_call(
        exchange_kernel,
        out_shape=[jax.ShapeDtypeStruct(shape, F32)] * 2,
        compiler_params=VMEM,
        cost_estimate=FREE,
    )(own, near, far)


def opposite_kernel(slabs, *refs):
    n = len(slabs)
    before_ref, mine_ref, other_ref, total_ref = refs[n + 2 :]
    step = pl.program_id(0)

    @pl.when(step == 0)
    def _():
        total_ref[...] = before_ref[...]

    add_step(slabs, refs[:n], refs[n], refs[n + 1], total_ref)

    @pl.when(step == pl.num_programs(0) - 1)
    def _():
        core = lax.rem(lax.axis_index("cd"), CORES)
        for slab in range(2):
            lay_out(total_ref, 32 * slab, slab, lambda layer: layer, core, mine_ref, other_ref)


def opposite_sums(pieces, slabs, weights, integrals, first, before):
    n, (rows, pairs) = len(pieces), pieces[0].shape
    columns = integrals.shape[1]
    return pl.pallas_call(
        functools.partial(opposite_kernel, slabs),
        grid=(pairs // STEP,),
        in_specs=specs([pl.BlockSpec((rows, STEP), lambda k: (0, k))] * n, columns, first)
        + [pl.BlockSpec(before.shape, lambda k: (0, 0))],
        out_specs=[pl.BlockSpec((LAYERS, 4, columns), lambda k: (0, 0, 0))] * 2,
        out_shape=[jax.ShapeDtypeStruct((LAYERS, 4, columns), F32)] * 2,
        scratch_shapes=[pltpu.VMEM((n * rows, columns), F32)],
        compiler_params=VMEM,
        cost_estimate=FREE,
    )(*pieces, weights, integrals, before)


def last_kernel(mine_ref, got_ref, mine_opposite_ref, got_opposite_ref, out_ref):
    group = lax.rem(lax.axis_index("ab") + 2, GROUPS)
    out_ref[...] = mine_ref[...] + got_ref[...]
    for layer in range(LAYERS):
        out_ref[place(layer, group)] = mine_opposite_ref[layer] + got_opposite_ref[layer]


def last_sums(*arrays):
    return pl.pallas_call(
        last_kernel,
        out_shape=jax.ShapeDtypeStruct(arrays[0].shape, F32),
        compiler_params=VMEM,
        cost_estimate=FREE,
    )(*arrays)


def finish_kernel(shares_ref, a_ref, b_ref, out_ref):
    keep = jnp.where(a_ref[...] == b_ref[...], F32(0.0), F32(0.5))
    summed = jnp.sum(shares_ref[...], axis=0)
    out_ref[:, 0, :] = 0.5 * summed[0:2]
    out_ref[:, 1, :] = keep * summed[2:4]


def pieces_kernel(own_ref, *refs):
    plus_ref, minus_ref = refs[-2:]
    plus_ref[...] = own_ref[0]
    minus_ref[...] = own_ref[1]


def slabs_after(amplitudes, pairs, *after):
    rows = amplitudes.shape[1]
    return pl.pallas_call(
        pieces_kernel,
        grid=(pairs // STEP,),
        in_specs=[pl.BlockSpec((2, rows, STEP), lambda k: (0, 0, k))] + [pl.BlockSpec(memory_space=pl.ANY)] * len(after),
        out_specs=[pl.BlockSpec((rows, STEP), lambda k: (0, k))] * 2,
        out_shape=[jax.ShapeDtypeStruct((rows, pairs), F32)] * 2,
        compiler_params=VMEM,
        cost_estimate=FREE,
    )(amplitudes, *after)


def right(x):
    return lax.ppermute(x, "ab", [(i, (i + 1) % GROUPS) for i in range(GROUPS)])


def left(x):
    return lax.ppermute(x, "ab", [(i, (i - 1) % GROUPS) for i in range(GROUPS)])


def over_cores(x):
    return lax.ppermute(x, "cd", [(i, i ^ 1) for i in range(GROUPS * LAYERS * CORES)])


def local(amplitudes, integrals, c_index, d_index, a_index, b_index):
    pairs, columns = integrals.shape
    cut = pairs - STEP

    same = c_index == d_index
    weights = jnp.stack([jnp.where(same, F32(0.5), F32(1.0)), jnp.where(same, F32(0.0), F32(1.0))])

    right_last, left_last = right(amplitudes[0, :, cut:]), left(amplitudes[1, :, cut:])
    plus, minus = slabs_after(amplitudes, cut)
    right_plus, left_minus = right(plus), left(minus)
    own = own_sums(amplitudes, weights, integrals, (right_last, left_last))
    plus, minus = slabs_after(amplitudes, pairs, own)
    right_minus, left_plus = right(minus), left(plus)
    onward = [right(right_plus), left(left_minus)]
    onward_last = [right(right_last), left(left_last)]

    near = partial_sums([right_plus, left_minus], (0, 1), weights, integrals)
    near = partial_sums([right_last, left_last], (0, 1), weights, integrals, cut // STEP) + near
    far = partial_sums([right_minus, left_plus], (1, 0), weights, integrals)
    mine, other = exchange(own, near, far)
    got = over_cores(other)
    opposite = partial_sums(onward, (0, 1), weights, integrals, 0, (got,))
    mine_opposite, other = opposite_sums(onward_last, (0, 1), weights, integrals, cut // STEP, opposite)
    part_sum = last_sums(mine, got, mine_opposite, over_cores(other))

    planes = [
        [CORES * (LAYERS * group + layer) + core for layer in ORDER for group in reversed(range(GROUPS))] for core in range(CORES)
    ]
    shares = lax.all_to_all(part_sum, "cd", 0, 0, tiled=True, axis_index_groups=planes)
    return pl.pallas_call(
        finish_kernel, out_shape=jax.ShapeDtypeStruct((2, 2, columns), F32), compiler_params=VMEM, cost_estimate=FREE
    )(shares, a_index.reshape(1, columns), b_index.reshape(1, columns))


def solution(mesh):
    placed = (P(None, "ab", "cd"), P("cd", "ab"), P("cd"), P("cd"), P("ab"), P("ab"))
    return jax.shard_map(local, mesh=mesh, in_specs=placed, out_specs=P("cd", None, "ab"), check_vma=False)
```
